32 devices in a mesh: ctx: 8 (over y, x, core), head: 4 (over z).
Axes of the slice: x: 2, y: 2, z: 4, core: 2. Of those that a mesh axis runs over, the one named last changes fastest.
Arguments:
- query: bfloat16 [4096, 4096], P(('ctx', 'head')), may hold values from -12 to 12
- key: bfloat16 [4096, 1024], P(('ctx', 'head')), may hold values from -4 to 4
- value: bfloat16 [4096, 1024], P(('ctx', 'head')), may hold values from -5 to 5
- d_out: bfloat16 [4096, 4096], P(('ctx', 'head')), may hold values from -5 to 5
- stretch_ids: int32 [16], replicated, may hold values from 0 to 15, as said below
Outputs:
- grad_query: bfloat16 [4096, 4096], P(('ctx', 'head'))
- grad_key: bfloat16 [4096, 1024], P(('ctx', 'head'))
- grad_value: bfloat16 [4096, 1024], P(('ctx', 'head'))
The draws below stay inside these ranges and needn't reach their ends.
Inputs may be any that keep to these rules, and one draw needn't show every extreme that they name: `stretch_ids`: a permutation in which slots 2r and 2r+1 hold blocks c and 15 - c for some c, in either order.
All inputs are finite; a program needn't handle non-finite values.
Results may differ from the reference program's by a relative error of at most 0.028.
Values may be sent and summed in bfloat16 or wider, within the bound.
No kernel may reach another device: no remote copies, remote signals or barrier semaphores. Data moves between devices by JAX's collectives and lax.ppermute only.
A program may use at most 128 MiB of HBM per device.

```python
import jax
import jax.numpy as jnp
from jax import lax

QUERY_HEAD_COUNT = 32
KEY_VALUE_HEADS = 8
HEAD_SIZE = 128
WINDOW = 4
SEQUENCE_TOKENS = 4096
ROWS = 512
STRETCH = 256
N_CTX = 8


def draw_query(key, part):
    value_rows = jnp.clip(jax.random.normal(jax.random.fold_in(key, 3), (SEQUENCE_TOKENS, QUERY_HEAD_COUNT * HEAD_SIZE)), -4.0, 4.0)
    return value_rows.astype(jnp.bfloat16)


def draw_key(key, part):
    value_rows = jnp.clip(jax.random.normal(jax.random.fold_in(key, 13), (SEQUENCE_TOKENS, KEY_VALUE_HEADS * HEAD_SIZE)), -4.0, 4.0)
    return value_rows.astype(jnp.bfloat16)


def draw_stretch_ids(key, part):
    order = jax.random.permutation(jax.random.fold_in(key, 21), N_CTX).astype(jnp.int32)
    flips = jax.random.randint(jax.random.fold_in(key, 22), (N_CTX,), 0, 2)
    first = jnp.where(flips == 1, 2 * N_CTX - 1 - order, order)
    second = 2 * N_CTX - 1 - first
    return jnp.stack((first, second), axis=1).reshape(2 * N_CTX).astype(jnp.int32)


def block_scale(key, dims, cuts, smallest, top_value):
    factor_of = 1.0
    for dim, blocks in cuts:
        draws = jax.random.uniform(jax.random.fold_in(jax.random.fold_in(key, 6), dim), (blocks,), jnp.float32, smallest / len(cuts), top_value / len(cuts))
        factor_of = factor_of * jnp.repeat(jnp.exp(draws), dims[dim] // blocks).reshape((-1,) + (1,) * (len(dims) - 1 - dim))
    return factor_of


def noise(rng, shape, scale, limit, split=(), kind=jnp.bfloat16):
    values = jax.random.normal(rng, shape, jnp.float32) * scale
    if len(split) > 0:
        values = block_scale(rng, shape, split, -0.22, 0.18) * values
    return jnp.clip(values, min=-limit, max=limit).astype(kind)


def setup_inputs(seed: int = 0) -> dict:
    key_of = jax.random.split(jax.random.key(seed), 6)
    return {
        "query": draw_query(jax.random.fold_in(key_of[5], 71), 0),
        "key": draw_key(jax.random.fold_in(key_of[5], 71), 0),
        "value": noise(key_of[2], (SEQUENCE_TOKENS, KEY_VALUE_HEADS * HEAD_SIZE), 1.0, 5.0, ((0, 32),)),
        "d_out": noise(key_of[3], (SEQUENCE_TOKENS, QUERY_HEAD_COUNT * HEAD_SIZE), 1.0, 5.0, ((0, 32),)),
        "stretch_ids": draw_stretch_ids(jax.random.fold_in(key_of[5], 71), 0),
    }


def reference(query, key, value, d_out, stretch_ids):
    rank_index = jnp.arange(SEQUENCE_TOKENS, dtype=jnp.int32)
    position = stretch_ids[rank_index // STRETCH].astype(jnp.int32) * STRETCH + rank_index % STRETCH
    scale = HEAD_SIZE ** -0.5
    group_width = QUERY_HEAD_COUNT // KEY_VALUE_HEADS
    query_heads = query.reshape(SEQUENCE_TOKENS, QUERY_HEAD_COUNT, HEAD_SIZE).transpose(1, 0, 2)
    grad_heads = d_out.reshape(SEQUENCE_TOKENS, QUERY_HEAD_COUNT, HEAD_SIZE).transpose(1, 0, 2)
    key_head_rows = jnp.repeat(key.reshape(SEQUENCE_TOKENS, KEY_VALUE_HEADS, HEAD_SIZE).transpose(1, 0, 2), group_width, axis=0)
    value_head_rows = jnp.repeat(value.reshape(SEQUENCE_TOKENS, KEY_VALUE_HEADS, HEAD_SIZE).transpose(1, 0, 2), group_width, axis=0)
    local = jnp.arange(ROWS, dtype=jnp.int32)
    offsets = jnp.arange(WINDOW, dtype=jnp.int32)

    def one_head(operands):
        q_all, g_all, k_all, v_all = operands

        def one_rank(carry, rank):
            grad_k_acc, grad_v_acc = carry
            q_rows = rank * ROWS + local
            k_rows = ((((rank - offsets) % N_CTX) * ROWS)[:, None] + local[None, :]).reshape(WINDOW * ROWS).astype(jnp.int32)
            q_one = q_all[q_rows]
            g_one = g_all[q_rows]
            k_one = k_all[k_rows]
            v_one = v_all[k_rows]
            visible = position[q_rows][:, None] >= position[k_rows][None, :]
            logits = jnp.dot(q_one, k_one.T, preferred_element_type=jnp.float32) * scale
            logits = jnp.where(visible, logits, -jnp.inf)
            top = jnp.max(logits, axis=1)
            log_total = top + jnp.log(jnp.sum(jnp.exp(logits - top[:, None]), axis=1))
            probs = jnp.exp(logits - log_total[:, None])
            probs_low = probs.astype(jnp.bfloat16)
            attn_out = jnp.dot(probs_low, v_one, preferred_element_type=jnp.float32)
            row_dot = jnp.sum(g_one.astype(jnp.float32) * attn_out, axis=1)
            value_gradient = jnp.dot(probs_low.T, g_one, preferred_element_type=jnp.float32)
            grad_p = jnp.dot(g_one, v_one.T, preferred_element_type=jnp.float32)
            grad_s = (probs * (grad_p - row_dot[:, None]) * scale).astype(jnp.bfloat16)
            grad_q = jnp.dot(grad_s, k_one, preferred_element_type=jnp.float32)
            key_gradient = jnp.dot(grad_s.T, q_one, preferred_element_type=jnp.float32)
            grad_k_acc = grad_k_acc.at[k_rows].add(key_gradient)
            grad_v_acc = grad_v_acc.at[k_rows].add(value_gradient)
            return (grad_k_acc, grad_v_acc), grad_q.astype(jnp.bfloat16)

        start = (jnp.zeros((SEQUENCE_TOKENS, HEAD_SIZE), jnp.float32), jnp.zeros((SEQUENCE_TOKENS, HEAD_SIZE), jnp.float32))
        (key_gradient, value_gradient), grad_q = lax.scan(one_rank, start, jnp.arange(N_CTX, dtype=jnp.int32))
        return grad_q.reshape(SEQUENCE_TOKENS, HEAD_SIZE), key_gradient, value_gradient

    grad_q, key_gradient, value_gradient = lax.map(one_head, (query_heads, grad_heads, key_head_rows, value_head_rows))
    key_gradient = jnp.sum(key_gradient.reshape(KEY_VALUE_HEADS, group_width, SEQUENCE_TOKENS, HEAD_SIZE), axis=1)
    value_gradient = jnp.sum(value_gradient.reshape(KEY_VALUE_HEADS, group_width, SEQUENCE_TOKENS, HEAD_SIZE), axis=1)
    out_q = grad_q.transpose(1, 0, 2).reshape(SEQUENCE_TOKENS, QUERY_HEAD_COUNT * HEAD_SIZE)
    key_output = key_gradient.transpose(1, 0, 2).reshape(SEQUENCE_TOKENS, KEY_VALUE_HEADS * HEAD_SIZE).astype(jnp.bfloat16)
    value_output = value_gradient.transpose(1, 0, 2).reshape(SEQUENCE_TOKENS, KEY_VALUE_HEADS * HEAD_SIZE).astype(jnp.bfloat16)
    return (out_q, key_output, value_output)
```

```python
import jax
import jax.numpy as jnp
from jax import lax
from jax.experimental import pallas as pl
from jax.experimental.pallas import tpu as pltpu
from jax.sharding import PartitionSpec as P

QUERY_HEAD_COUNT = 32
KEY_VALUE_HEADS = 8
HEAD_SIZE = 128
WINDOW = 4
SCALE = HEAD_SIZE ** (-0.5)
LOG2_E = 1.4426950408889634
NT = (((1,), (1,)), ((), ()))
NN = (((1,), (0,)), ((), ()))
TN = (((0,), (0,)), ((), ()))


def dot(a, b, dims):
    return lax.dot_general(a, b, dims, preferred_element_type=jnp.float32)


def fold(x, op):
    return op(x.reshape(x.shape[0] // 8, 8, x.shape[1]), axis=0)


def attention_kernel(
    ranks, splits, heads, rows,
    ids_ref, q_ref, g_ref, kv_ref, dq_ref, dkv_ref,
    tile_ref, st_ref, dp_ref, dqt_ref, dk_ref, dv_ref,
):
    rank = pl.program_id(0)
    z = ids_ref[2 * ranks]
    half = splits // 2
    slot = z // half
    own = ids_ref[2 * rank + slot]

    @pl.when(rank == 0)
    def _():
        dk_ref[...] = jnp.zeros_like(dk_ref)
        dv_ref[...] = jnp.zeros_like(dv_ref)

    count = jnp.int32(0)
    for back in range(WINDOW):
        key_rank = lax.rem(rank - back + ranks, ranks)
        for key_slot in range(2):
            tile_ref[count] = key_rank * 2 + key_slot
            count = count + jnp.where(ids_ref[2 * key_rank + key_slot] < own, 1, 0)

    def stack(ref):
        return jnp.concatenate(
            [ref[0, :, h * HEAD_SIZE : (h + 1) * HEAD_SIZE] for h in range(heads)], axis=0
        )

    qs = stack(q_ref)
    gs = stack(g_ref)

    def keys(which, key_rank, key_slot):
        return jnp.concatenate(
            [kv_ref[key_slot * half + i, which, key_rank] for i in range(half)], axis=0
        )

    def place(i):
        t = tile_ref[i]
        return t // 2, lax.rem(t, 2)

    width = heads * rows
    key_pos = lax.broadcasted_iota(jnp.int32, (half * rows, width), 0)
    row_pos = lax.rem(lax.broadcasted_iota(jnp.int32, (half * rows, width), 1), rows)
    row_pos = row_pos + lax.rem(z, half) * rows

    s_own = jnp.where(key_pos <= row_pos, dot(keys(0, rank, slot), qs, NT), -1e30)
    st_ref[0] = s_own

    def scores(i, top):
        s = dot(keys(0, *place(i)), qs, NT)
        st_ref[i + 1] = s
        return jnp.maximum(top, fold(s, jnp.max))

    top = lax.fori_loop(0, count, scores, fold(s_own, jnp.max))
    top = jnp.max(top, axis=0, keepdims=True) * (SCALE * LOG2_E)

    def weights(i, total):
        p = jnp.exp2(st_ref[i] * (SCALE * LOG2_E) - top)
        st_ref[i] = p
        return total + fold(p, jnp.sum)

    total = lax.fori_loop(0, count + 1, weights, jnp.zeros((8, width), jnp.float32))
    inverse = 1.0 / jnp.sum(total, axis=0, keepdims=True)

    def add(ref, key_rank, key_slot, update):
        for i in range(half):
            ref[key_slot * half + i, key_rank] += update[i * rows : (i + 1) * rows]

    def values(i, key_rank, key_slot, delta):
        p = st_ref[i] * inverse
        st_ref[i] = p
        dp = dot(keys(1, key_rank, key_slot), gs, NT)
        dp_ref[i] = dp
        add(dv_ref, key_rank, key_slot, dot(p.astype(jnp.bfloat16), gs, NN))
        return delta + fold(p * dp, jnp.sum)

    delta = values(0, rank, slot, jnp.zeros((8, width), jnp.float32))
    delta = lax.fori_loop(0, count, lambda i, d: values(i + 1, *place(i), d), delta)
    delta = jnp.sum(delta, axis=0, keepdims=True)

    def grads(i, key_rank, key_slot):
        ds = (st_ref[i] * (dp_ref[i] - delta)).astype(jnp.bfloat16)
        add(dk_ref, key_rank, key_slot, dot(ds, qs, NN))
        return dot(keys(0, key_rank, key_slot), ds, TN)

    dqt_ref[...] = grads(0, rank, slot)

    def others(i, carry):
        dqt_ref[...] += grads(i + 1, *place(i))
        return carry

    lax.fori_loop(0, count, others, 0)
    dq = (dqt_ref[...] * SCALE).T.astype(jnp.bfloat16)
    for h in range(heads):
        dq_ref[0, :, h * HEAD_SIZE : (h + 1) * HEAD_SIZE] = dq[h * rows : (h + 1) * rows]

    @pl.when(rank == ranks - 1)
    def _():
        dkv_ref[:, 0] = (dk_ref[...] * SCALE).astype(jnp.bfloat16)
        dkv_ref[:, 1] = dv_ref[...].astype(jnp.bfloat16)


def attention(ids, q, g, kv):
    ranks, rows, width = q.shape
    splits = kv.shape[0]
    heads = width // HEAD_SIZE
    stretch = splits // 2 * rows
    tiles = 2 * WINDOW
    row_block = pl.BlockSpec((1, rows, width), lambda r: (r, 0, 0))
    whole = pl.BlockSpec(kv.shape, lambda r: (0, 0, 0, 0, 0), pipeline_mode=pl.Buffered(1))
    flops = 10 * ranks * 5 * stretch * heads * rows * HEAD_SIZE

    def kernel(*refs):
        attention_kernel(ranks, splits, heads, rows, *refs)

    return pl.pallas_call(
        kernel,
        grid=(ranks,),
        in_specs=[pl.BlockSpec(memory_space=pltpu.SMEM), row_block, row_block, whole],
        out_specs=(row_block, whole),
        out_shape=(
            jax.ShapeDtypeStruct(q.shape, jnp.bfloat16),
            jax.ShapeDtypeStruct(kv.shape, jnp.bfloat16),
        ),
        scratch_shapes=[
            pltpu.SMEM((tiles + 1,), jnp.int32),
            pltpu.VMEM((tiles + 1, stretch, heads * rows), jnp.float32),
            pltpu.VMEM((tiles + 1, stretch, heads * rows), jnp.float32),
            pltpu.VMEM((HEAD_SIZE, heads * rows), jnp.float32),
            pltpu.VMEM((splits, ranks, rows, HEAD_SIZE), jnp.float32),
            pltpu.VMEM((splits, ranks, rows, HEAD_SIZE), jnp.float32),
        ],
        compiler_params=pltpu.CompilerParams(vmem_limit_bytes=60 * 1024 * 1024),
        cost_estimate=pl.CostEstimate(flops=flops, bytes_accessed=10 * q.size, transcendentals=0),
    )(ids, q, g, kv)


def body(query, key, value, d_out, stretch_ids):
    rows = query.shape[0]
    ranks = lax.axis_size("ctx")
    copies = ranks // KEY_VALUE_HEADS
    z = lax.axis_index("head")

    def by_device(array):
        return array.reshape(rows, ranks, array.shape[1] // ranks).swapaxes(0, 1)

    def to_heads(array):
        return lax.all_to_all(array, "ctx", split_axis=0, concat_axis=0, tiled=True)

    def by_key_head(array):
        split = array.reshape(rows, KEY_VALUE_HEADS, HEAD_SIZE).swapaxes(0, 1)
        return jnp.repeat(split, copies, axis=0)

    kv = to_heads(jnp.stack((by_key_head(key), by_key_head(value)), axis=1)).swapaxes(0, 1)
    kv = lax.all_gather(kv, "head", axis=0, tiled=False)
    q = to_heads(by_device(query))
    g = to_heads(by_device(d_out))
    ids = jnp.concatenate((stretch_ids, z.astype(jnp.int32)[None]))
    dq, dkv = attention(ids, q, g, kv)
    dq = to_heads(dq).swapaxes(0, 1).reshape(rows, QUERY_HEAD_COUNT * HEAD_SIZE)
    dkv = lax.psum_scatter(dkv, "head", scatter_dimension=0, tiled=False)
    dkv = lax.all_to_all(dkv, "ctx", split_axis=1, concat_axis=1, tiled=True)
    if copies > 1:
        shape = (2, KEY_VALUE_HEADS, copies, rows, HEAD_SIZE)
        dkv = jnp.sum(dkv.reshape(shape).astype(jnp.float32), axis=2).astype(jnp.bfloat16)
    dkv = dkv.swapaxes(1, 2).reshape(2, rows, KEY_VALUE_HEADS * HEAD_SIZE)
    return dq, dkv[0], dkv[1]


def solution(mesh):
    spec = P(("ctx", "head"), None)
    return jax.shard_map(
        body,
        mesh=mesh,
        in_specs=(spec, spec, spec, spec, P()),
        out_specs=(spec, spec, spec),
        check_vma=False,
    )
```

```python
import jax
import jax.numpy as jnp
from jax import lax
from jax.experimental import pallas as pl
from jax.experimental.pallas import tpu as pltpu
from jax.sharding import PartitionSpec as P

QUERY_HEAD_COUNT = 32
KEY_VALUE_HEADS = 8
HEAD_SIZE = 128
WINDOW = 4
TILES = 2 * WINDOW
SCALE = HEAD_SIZE ** (-0.5)
LOG2_E = 1.4426950408889634
NT = (((1,), (1,)), ((), ()))
NN = (((1,), (0,)), ((), ()))
TN = (((0,), (0,)), ((), ()))
LOW = jnp.bfloat16
VMEM_LIMIT = 60 * 1024 * 1024


def dot(a, b, dims):
    return lax.dot_general(a, b, dims, preferred_element_type=jnp.float32)


def fold(x, op):
    return op(x.reshape(x.shape[0] // 8, 8, x.shape[1]), axis=0)


def stack(ref):
    heads = ref.shape[2] // HEAD_SIZE
    return jnp.concatenate(
        [ref[0, :, h * HEAD_SIZE : (h + 1) * HEAD_SIZE] for h in range(heads)], axis=0
    )


def list_tiles(ids_ref, tile_ref, ranks, splits):
    rank = pl.program_id(0)
    slot = ids_ref[2 * ranks] // (splits // 2)
    own = ids_ref[2 * rank + slot]
    tile_ref[0] = rank * 2 + slot
    count = jnp.int32(1)
    for back in range(WINDOW):
        key_rank = lax.rem(rank - back + ranks, ranks)
        for key_slot in range(2):
            tile_ref[count] = key_rank * 2 + key_slot
            count = count + jnp.where(ids_ref[2 * key_rank + key_slot] < own, 1, 0)
    return count


def load_chunks(ids_ref, chunk_refs, all_ref, sem_ref, ranks, splits):
    z = ids_ref[2 * ranks]
    return [
        pltpu.make_async_copy(
            chunk, all_ref.at[lax.rem(z - s + splits, splits)], sem_ref.at[s]
        )
        for s, chunk in enumerate(chunk_refs)
    ]


def tile_rows(all_ref, tile_ref, i, half):
    t = tile_ref[i]
    return jnp.concatenate(
        [all_ref[lax.rem(t, 2) * half + j, t // 2] for j in range(half)], axis=0
    )


def add_tile(all_ref, tile_ref, i, half, rows, update):
    t = tile_ref[i]
    for j in range(half):
        all_ref[lax.rem(t, 2) * half + j, t // 2] += update[j * rows : (j + 1) * rows]


def probs_kernel(ranks, splits, heads, rows, ids_ref, q_ref, *refs):
    k_chunks, (p_ref, tile_ref, st_ref, k_ref, sem_ref) = refs[:splits], refs[splits:]
    half = splits // 2
    width = heads * rows

    @pl.when(pl.program_id(0) == 0)
    def _():
        copies = load_chunks(ids_ref, k_chunks, k_ref, sem_ref, ranks, splits)
        for copy in copies:
            copy.start()
        for copy in copies:
            copy.wait()

    count = list_tiles(ids_ref, tile_ref, ranks, splits)
    qs = stack(q_ref)
    key_pos = lax.broadcasted_iota(jnp.int32, (half * rows, width), 0)
    row_pos = lax.rem(lax.broadcasted_iota(jnp.int32, (half * rows, width), 1), rows)
    row_pos = row_pos + lax.rem(ids_ref[2 * ranks], half) * rows
    s_own = jnp.where(
        key_pos <= row_pos, dot(tile_rows(k_ref, tile_ref, 0, half), qs, NT), -1e30
    )
    st_ref[0] = s_own

    def scores(i, top):
        s = dot(tile_rows(k_ref, tile_ref, i, half), qs, NT)
        st_ref[i] = s
        return jnp.maximum(top, fold(s, jnp.max))

    top = lax.fori_loop(1, count, scores, fold(s_own, jnp.max))
    top = jnp.max(top, axis=0, keepdims=True) * (SCALE * LOG2_E)

    def weights(i, total):
        p = jnp.exp2(st_ref[i] * (SCALE * LOG2_E) - top)
        st_ref[i] = p
        return total + fold(p, jnp.sum)

    total = lax.fori_loop(0, count, weights, jnp.zeros((8, width), jnp.float32))
    inverse = 1.0 / jnp.sum(total, axis=0, keepdims=True)

    def normal(i, carry):
        p_ref[0, i] = (st_ref[i] * inverse).astype(LOW)
        return carry

    lax.fori_loop(0, count, normal, 0)


def value_kernel(ranks, splits, heads, rows, ids_ref, g_ref, p_ref, *refs):
    out_refs, (tile_ref, dv_ref) = refs[:splits], refs[splits:]
    half = splits // 2

    @pl.when(pl.program_id(0) == 0)
    def _():
        dv_ref[...] = jnp.zeros_like(dv_ref)

    count = list_tiles(ids_ref, tile_ref, ranks, splits)
    gs = stack(g_ref)

    def values(i, carry):
        add_tile(dv_ref, tile_ref, i, half, rows, dot(p_ref[0, i], gs, NN))
        return carry

    lax.fori_loop(0, count, values, 0)

    @pl.when(pl.program_id(0) == ranks - 1)
    def _():
        z = ids_ref[2 * ranks]
        for s, out in enumerate(out_refs):
            out[...] = dv_ref[lax.rem(z + s, splits)].astype(LOW)


def grads_kernel(ranks, splits, heads, rows, ids_ref, q_ref, g_ref, p_ref, *refs):
    k_chunks, v_chunks, dq_ref = refs[:splits], refs[splits : 2 * splits], refs[2 * splits]
    out_refs = refs[2 * splits + 1 : 3 * splits + 1]
    tile_ref, dp_ref, dqt_ref, k_ref, v_ref, dk_ref, sem_ref = refs[3 * splits + 1 :]
    half = splits // 2
    width = heads * rows

    @pl.when(pl.program_id(0) == 0)
    def _():
        copies = load_chunks(ids_ref, k_chunks, k_ref, sem_ref.at[0], ranks, splits)
        copies += load_chunks(ids_ref, v_chunks, v_ref, sem_ref.at[1], ranks, splits)
        for copy in copies:
            copy.start()
        dk_ref[...] = jnp.zeros_like(dk_ref)
        for copy in copies:
            copy.wait()

    count = list_tiles(ids_ref, tile_ref, ranks, splits)
    qs = stack(q_ref)
    gs = stack(g_ref)

    def deltas(i, delta):
        dp = dot(tile_rows(v_ref, tile_ref, i, half), gs, NT)
        dp_ref[i] = dp
        return delta + fold(p_ref[0, i].astype(jnp.float32) * dp, jnp.sum)

    delta = lax.fori_loop(0, count, deltas, jnp.zeros((8, width), jnp.float32))
    delta = jnp.sum(delta, axis=0, keepdims=True)
    dqt_ref[...] = jnp.zeros_like(dqt_ref)

    def grads(i, carry):
        ds = (p_ref[0, i].astype(jnp.float32) * (dp_ref[i] - delta)).astype(LOW)
        add_tile(dk_ref, tile_ref, i, half, rows, dot(ds, qs, NN))
        dqt_ref[...] += dot(tile_rows(k_ref, tile_ref, i, half), ds, TN)
        return carry

    lax.fori_loop(0, count, grads, 0)
    dq = (dqt_ref[...] * SCALE).T.astype(LOW)
    for h in range(heads):
        dq_ref[0, :, h * HEAD_SIZE : (h + 1) * HEAD_SIZE] = dq[h * rows : (h + 1) * rows]

    @pl.when(pl.program_id(0) == ranks - 1)
    def _():
        z = ids_ref[2 * ranks]
        for s, out in enumerate(out_refs):
            out[...] = (dk_ref[lax.rem(z + s, splits)] * SCALE).astype(LOW)


class Attention:
    def __init__(self, ids, q, splits):
        self.ids, self.splits = ids, splits
        self.ranks, self.rows, self.width = q.shape
        self.heads = self.width // HEAD_SIZE
        self.stretch = splits // 2 * self.rows
        self.chunk = (self.ranks, self.rows, HEAD_SIZE)
        self.smem = pl.BlockSpec(memory_space=pltpu.SMEM)
        self.any = pl.BlockSpec(memory_space=pl.ANY)
        self.row_block = pl.BlockSpec((1, self.rows, self.width), lambda r: (r, 0, 0))
        self.probs_shape = (self.ranks, TILES, self.stretch, self.heads * self.rows)
        self.probs_block = pl.BlockSpec((1,) + self.probs_shape[1:], lambda r: (r, 0, 0, 0))
        self.chunk_block = pl.BlockSpec(
            self.chunk, lambda r: (0, 0, 0), pipeline_mode=pl.Buffered(1)
        )
        self.chunk_out = jax.ShapeDtypeStruct(self.chunk, LOW)
        self.tile_list = pltpu.SMEM((TILES + 1,), jnp.int32)
        self.scores = pltpu.VMEM(self.probs_shape[1:], jnp.float32)
        self.all_low = pltpu.VMEM((splits,) + self.chunk, LOW)
        self.all_wide = pltpu.VMEM((splits,) + self.chunk, jnp.float32)

    def call(self, kernel, matmuls, *operands, **kwargs):
        def bound(*refs):
            kernel(self.ranks, self.splits, self.heads, self.rows, *refs)

        tile = 2 * self.stretch * self.heads * self.rows * HEAD_SIZE
        cost = pl.CostEstimate(
            flops=matmuls * 5 * self.ranks * tile, bytes_accessed=1 << 24, transcendentals=0
        )
        return pl.pallas_call(
            bound,
            grid=(self.ranks,),
            compiler_params=pltpu.CompilerParams(vmem_limit_bytes=VMEM_LIMIT),
            cost_estimate=cost,
            **kwargs,
        )(self.ids, *operands)

    def probs(self, q, k):
        return self.call(
            probs_kernel, 4, q, *k,
            in_specs=[self.smem, self.row_block] + [self.any] * self.splits,
            out_specs=self.probs_block,
            out_shape=jax.ShapeDtypeStruct(self.probs_shape, LOW),
            scratch_shapes=[
                self.tile_list, self.scores, self.all_low,
                pltpu.SemaphoreType.DMA((self.splits,)),
            ],
        )

    def value_grads(self, g, p):
        return self.call(
            value_kernel, 2, g, p,
            in_specs=[self.smem, self.row_block, self.probs_block],
            out_specs=[self.chunk_block] * self.splits,
            out_shape=[self.chunk_out] * self.splits,
            scratch_shapes=[self.tile_list, self.all_wide],
        )

    def grads(self, q, g, p, k, v):
        out = self.call(
            grads_kernel, 4, q, g, p, *k, *v,
            in_specs=[self.smem, self.row_block, self.row_block, self.probs_block]
            + [self.any] * (2 * self.splits),
            out_specs=[self.row_block] + [self.chunk_block] * self.splits,
            out_shape=[jax.ShapeDtypeStruct(q.shape, LOW)] + [self.chunk_out] * self.splits,
            scratch_shapes=[
                self.tile_list, self.scores,
                pltpu.VMEM((HEAD_SIZE, self.heads * self.rows), jnp.float32),
                self.all_low, self.all_low, self.all_wide,
                pltpu.SemaphoreType.DMA((2, self.splits)),
            ],
        )
        return out[0], out[1:]


def body(query, key, value, d_out, stretch_ids):
    rows = query.shape[0]
    ranks = lax.axis_size("ctx")
    splits = lax.axis_size("head")
    copies = ranks // KEY_VALUE_HEADS
    z = lax.axis_index("head")

    def by_device(array):
        return array.reshape(rows, ranks, array.shape[1] // ranks).swapaxes(0, 1)

    def to_heads(array):
        return lax.all_to_all(array, "ctx", split_axis=0, concat_axis=0, tiled=True)

    def by_key_head(array):
        split = array.reshape(rows, KEY_VALUE_HEADS, HEAD_SIZE).swapaxes(0, 1)
        return jnp.repeat(split, copies, axis=0)

    def shift(array, by):
        return lax.ppermute(array, "head", [(i, (i + by) % splits) for i in range(splits)])

    def gather(array):
        return [array] + [shift(array, s) for s in range(1, splits)]

    def scatter(chunks):
        total = chunks[0].astype(jnp.float32)
        for s in range(1, splits):
            total = total + shift(chunks[s], s).astype(jnp.float32)
        return total.astype(LOW)

    kv = to_heads(jnp.stack((by_key_head(key), by_key_head(value)), axis=1))
    ids = jnp.concatenate((stretch_ids, z.astype(jnp.int32)[None]))
    q_in, k_own, v_own = lax.optimization_barrier((by_device(query), kv[:, 0], kv[:, 1]))
    k = gather(k_own)
    q, g_in = lax.optimization_barrier((to_heads(q_in), by_device(d_out)))
    k, v_own = lax.optimization_barrier((k, v_own))
    v = gather(v_own)
    g = to_heads(g_in)
    part = Attention(ids, q, splits)
    p = part.probs(q, k)
    dv, q = lax.optimization_barrier((part.value_grads(g, p), q))
    dv = scatter(dv)
    dq, dk = part.grads(q, g, p, k, v)
    dk = scatter(dk)
    dq = to_heads(dq).swapaxes(0, 1).reshape(rows, QUERY_HEAD_COUNT * HEAD_SIZE)
    dkv = to_heads(jnp.stack((dk, dv), axis=1))
    if copies > 1:
        shape = (KEY_VALUE_HEADS, copies, 2, rows, HEAD_SIZE)
        dkv = jnp.sum(dkv.reshape(shape).astype(jnp.float32), axis=1).astype(LOW)
    dkv = dkv.transpose(1, 2, 0, 3).reshape(2, rows, KEY_VALUE_HEADS * HEAD_SIZE)
    return dq, dkv[0], dkv[1]


def solution(mesh):
    spec = P(("ctx", "head"), None)
    return jax.shard_map(
        body,
        mesh=mesh,
        in_specs=(spec, spec, spec, spec, P()),
        out_specs=(spec, spec, spec),
        check_vma=False,
    )
```

```python
import jax
import jax.numpy as jnp
from jax import lax
from jax.experimental import pallas as pl
from jax.experimental.pallas import tpu as pltpu
from jax.sharding import PartitionSpec as P

QUERY_HEAD_COUNT = 32
KEY_VALUE_HEADS = 8
GROUP = QUERY_HEAD_COUNT // KEY_VALUE_HEADS
HEAD_SIZE = 128
WINDOW = 4
TILES = 3 + 2 * (WINDOW - 1)
SCALE = HEAD_SIZE ** (-0.5)
LOG2_E = 1.4426950408889634
NT = (((1,), (1,)), ((), ()))
NN = (((1,), (0,)), ((), ()))
TN = (((0,), (0,)), ((), ()))
LOW = jnp.bfloat16
WIDE = jnp.float32
VMEM_LIMIT = 60 * 1024 * 1024
SCORE_BYTES = 24 * 1024 * 1024


def dot(a, b, dims):
    return lax.dot_general(a, b, dims, preferred_element_type=WIDE)


def fold(x, op):
    return op(x.reshape(x.shape[0] // 8, 8, x.shape[1]), axis=0)


def list_tiles(ids_ref, tile_ref):
    def slots(turn):
        first, second = ids_ref[2 * turn], ids_ref[2 * turn + 1]
        return jnp.where(first < second, 0, 1), jnp.minimum(first, second)

    def put(i, query_slot, turn, key_slot):
        tile_ref[3 * i] = query_slot
        tile_ref[3 * i + 1] = turn
        tile_ref[3 * i + 2] = key_slot

    low, stretch = slots(0)
    put(0, 0, 0, 0)
    put(1, 1, 0, 1)
    put(2, 1 - low, 0, low)
    for turn in range(1, WINDOW):
        key_low, key_stretch = slots(turn)
        later = stretch > key_stretch
        put(2 * turn + 1, 1 - low, turn, key_low)
        put(
            2 * turn + 2,
            jnp.where(later, low, 1 - low),
            turn,
            jnp.where(later, key_low, 1 - key_low),
        )


def attention_kernel(splits, heads, rows, at_once, head, ids_ref, *refs):
    chunk_ref, block_refs = refs[0], refs[1 : 1 + WINDOW]
    refs = refs[1 + WINDOW :]
    dq_out, dkv_outs = refs[0], refs[1 : 1 + WINDOW]
    (
        tile_ref, x_ref, kv_ref, qs_ref, gs_ref, st_ref, dp_ref, dqt_ref, dkv_ref,
        top_ref, total_ref, delta_ref, sem_ref,
    ) = refs[1 + WINDOW :]
    half = splits // 2
    stretch = half * rows
    width = at_once * stretch
    z = ids_ref[2 * WINDOW]
    step = pl.program_id(0) if heads > at_once else 0

    def place(block):
        return lax.rem(z - block + splits, splits)

    def lanes(h):
        return pl.ds(pl.multiple_of((step * at_once + h) * HEAD_SIZE, HEAD_SIZE), HEAD_SIZE)

    @pl.when(pl.program_id(0) == 0)
    def _():
        copies = [
            pltpu.make_async_copy(chunk_ref.at[s], x_ref.at[s], sem_ref.at[s])
            for s in range(splits)
        ]
        copies += [
            pltpu.make_async_copy(
                block.at[:, :, pl.ds(2 * head * HEAD_SIZE, 2 * HEAD_SIZE)],
                kv_ref.at[t],
                sem_ref.at[splits + t],
            )
            for t, block in enumerate(block_refs)
        ]
        for copy in copies:
            copy.start()
        list_tiles(ids_ref, tile_ref)
        dkv_ref[...] = jnp.zeros_like(dkv_ref)
        for copy in copies:
            copy.wait()

    for slot in range(2):
        for j in range(half):
            for h in range(at_once):
                at = pl.ds(h * stretch + j * rows, rows)
                qs_ref[slot, at] = x_ref[slot * half + j, 0, :, lanes(h)]
                gs_ref[slot, at] = x_ref[slot * half + j, 1, :, lanes(h)]

    def part(which):
        return pl.ds(which * HEAD_SIZE, HEAD_SIZE)

    def tile(i):
        return tile_ref[3 * i], tile_ref[3 * i + 1], tile_ref[3 * i + 2]

    def keys(which, turn, key_slot):
        return jnp.concatenate(
            [kv_ref[turn, place(key_slot * half + j), :, part(which)] for j in range(half)], axis=0
        )

    def add_keys(which, turn, key_slot, update):
        for j in range(half):
            at = place(key_slot * half + j)
            dkv_ref[turn, at, :, part(which)] += update[j * rows : (j + 1) * rows]

    key_pos = lax.broadcasted_iota(jnp.int32, (stretch, width), 0)
    row_pos = lax.rem(lax.broadcasted_iota(jnp.int32, (stretch, width), 1), stretch)
    for slot in range(2):
        s = jnp.where(key_pos <= row_pos, dot(keys(0, 0, slot), qs_ref[slot], NT), -1e30)
        st_ref[slot] = s
        top_ref[slot] = fold(s, jnp.max)

    def scores(i, carry):
        slot, turn, key_slot = tile(i)
        s = dot(keys(0, turn, key_slot), qs_ref[slot], NT)
        st_ref[i] = s
        top_ref[slot] = jnp.maximum(top_ref[slot], fold(s, jnp.max))
        return carry

    lax.fori_loop(2, TILES, scores, 0)
    top_ref[...] = jnp.broadcast_to(
        jnp.max(top_ref[...], axis=1, keepdims=True) * (SCALE * LOG2_E), top_ref.shape
    )
    total_ref[...] = jnp.zeros_like(total_ref)
    delta_ref[...] = jnp.zeros_like(delta_ref)
    dqt_ref[...] = jnp.zeros_like(dqt_ref)

    def weights(i, carry):
        slot, _, _ = tile(i)
        p = jnp.exp2(st_ref[i] * (SCALE * LOG2_E) - top_ref[slot, 0:1])
        st_ref[i] = p
        total_ref[slot] += fold(p, jnp.sum)
        return carry

    lax.fori_loop(0, TILES, weights, 0)
    total_ref[...] = jnp.broadcast_to(
        1.0 / jnp.sum(total_ref[...], axis=1, keepdims=True), total_ref.shape
    )

    def values(i, carry):
        slot, turn, key_slot = tile(i)
        p = st_ref[i] * total_ref[slot, 0:1]
        st_ref[i] = p
        dp = dot(keys(1, turn, key_slot), gs_ref[slot], NT)
        dp_ref[i] = dp
        add_keys(1, turn, key_slot, dot(p.astype(LOW), gs_ref[slot], NN))
        delta_ref[slot] += fold(p * dp, jnp.sum)
        return carry

    lax.fori_loop(0, TILES, values, 0)
    delta_ref[...] = jnp.broadcast_to(
        jnp.sum(delta_ref[...], axis=1, keepdims=True), delta_ref.shape
    )

    def grads(i, carry):
        slot, turn, key_slot = tile(i)
        ds = (st_ref[i] * (dp_ref[i] - delta_ref[slot, 0:1])).astype(LOW)
        add_keys(0, turn, key_slot, dot(ds, qs_ref[slot], NN))
        dqt_ref[slot] += dot(keys(0, turn, key_slot), ds, TN)
        return carry

    lax.fori_loop(0, TILES, grads, 0)

    for slot in range(2):
        dq = (dqt_ref[slot] * SCALE).T.astype(LOW)
        for j in range(half):
            for h in range(at_once):
                at = h * stretch + j * rows
                dq_out[slot * half + j, :, lanes(h)] = dq[at : at + rows]

    @pl.when(pl.program_id(0) == heads // at_once - 1)
    def _():
        for t, out in enumerate(dkv_outs):
            out[:, :, part(0)] = (dkv_ref[t, :, :, part(0)] * SCALE).astype(LOW)
            out[:, :, part(1)] = dkv_ref[t, :, :, part(1)].astype(LOW)


def attention(ids, chunk, blocks, head):
    splits, _, rows, lanes = chunk.shape
    heads = lanes // HEAD_SIZE
    stretch = splits // 2 * rows
    at_once = heads
    while 2 * TILES * 4 * stretch * stretch * at_once > SCORE_BYTES and at_once % 2 == 0:
        at_once //= 2
    width = at_once * stretch

    def kernel(*refs):
        attention_kernel(splits, heads, rows, at_once, head, *refs)

    def whole(shape):
        return pl.BlockSpec(shape, lambda i: (0,) * len(shape), pipeline_mode=pl.Buffered(1))

    dq_shape, dkv_shape = (splits, rows, lanes), (splits, rows, 2 * HEAD_SIZE)
    out = pl.pallas_call(
        kernel,
        grid=(heads // at_once,),
        in_specs=[pl.BlockSpec(memory_space=pltpu.SMEM)]
        + [pl.BlockSpec(memory_space=pl.ANY)] * (1 + WINDOW),
        out_specs=[whole(dq_shape)] + [whole(dkv_shape)] * WINDOW,
        out_shape=[jax.ShapeDtypeStruct(dq_shape, LOW)]
        + [jax.ShapeDtypeStruct(dkv_shape, LOW)] * WINDOW,
        scratch_shapes=[
            pltpu.SMEM((3 * TILES,), jnp.int32),
            pltpu.VMEM(chunk.shape, LOW),
            pltpu.VMEM((WINDOW, splits, rows, 2 * HEAD_SIZE), LOW),
            pltpu.VMEM((2, width, HEAD_SIZE), LOW),
            pltpu.VMEM((2, width, HEAD_SIZE), LOW),
            pltpu.VMEM((TILES, stretch, width), WIDE),
            pltpu.VMEM((TILES, stretch, width), WIDE),
            pltpu.VMEM((2, HEAD_SIZE, width), WIDE),
            pltpu.VMEM((WINDOW, splits, rows, 2 * HEAD_SIZE), WIDE),
            pltpu.VMEM((2, 8, width), WIDE),
            pltpu.VMEM((2, 8, width), WIDE),
            pltpu.VMEM((2, 8, width), WIDE),
            pltpu.SemaphoreType.DMA((splits + WINDOW,)),
        ],
        compiler_params=pltpu.CompilerParams(vmem_limit_bytes=VMEM_LIMIT),
        cost_estimate=pl.CostEstimate(
            flops=16 * 2 * 5 * TILES * stretch * stretch * heads * HEAD_SIZE // 4,
            bytes_accessed=1 << 22,
            transcendentals=0,
        ),
    )(ids, chunk, *blocks)
    return out[0], out[1:]


def in_columns(parts, z, places, outs):
    rows = parts[0].shape[-2]

    def kernel(z_ref, *refs):
        part_refs, out_refs = refs[: len(parts)], refs[len(parts) :]
        for index, part in enumerate(part_refs):
            for piece, out, column in places(z_ref[0], index, part):
                width = piece.shape[-1]
                start = pl.multiple_of(column * width, HEAD_SIZE)
                out_refs[out][:, pl.ds(start, width)] = piece

    size = sum(part.size for part in parts) // rows // outs
    return pl.pallas_call(
        kernel,
        in_specs=[pl.BlockSpec(memory_space=pltpu.SMEM)]
        + [pl.BlockSpec(memory_space=pltpu.VMEM)] * len(parts),
        out_specs=[pl.BlockSpec(memory_space=pltpu.VMEM)] * outs,
        out_shape=[jax.ShapeDtypeStruct((rows, size), LOW)] * outs,
        compiler_params=pltpu.CompilerParams(vmem_limit_bytes=VMEM_LIMIT),
    )(z.astype(jnp.int32)[None], *parts)


def body(query, key, value, d_out, stretch_ids):
    rows = query.shape[0]
    ranks = lax.axis_size("ctx")
    splits = lax.axis_size("head")
    local = KEY_VALUE_HEADS // splits
    z = lax.axis_index("head")
    rank = lax.axis_index("ctx")
    fence = lax.optimization_barrier

    def shift(array, axis, by):
        size = lax.axis_size(axis)
        return lax.ppermute(array, axis, [(i, (i + by) % size) for i in range(size)])

    def exchange(chunks, sign):
        return [chunks[0]] + [shift(chunks[s], "head", sign * s) for s in range(1, splits)]

    def swap(array):
        return lax.all_to_all(array, "head", split_axis=0, concat_axis=0, tiled=True)

    def ids_of(turn):
        source = lax.rem(rank - turn + ranks, ranks)
        return lax.dynamic_slice_in_dim(stretch_ids, 2 * source, 2)

    ids = jnp.concatenate([ids_of(t) for t in range(WINDOW)] + [z.astype(jnp.int32)[None]])

    def for_device_ahead(s):
        start = lax.rem(z + s, splits) * (local * HEAD_SIZE)
        ahead = [
            lax.dynamic_slice_in_dim(array, start, local * HEAD_SIZE, 1) for array in (key, value)
        ]
        return jnp.concatenate(
            [
                array[:, j * HEAD_SIZE : (j + 1) * HEAD_SIZE]
                for j in range(local)
                for array in ahead
            ],
            axis=1,
        )

    parts = exchange([for_device_ahead(s) for s in range(splits)], 1)
    both = [
        jnp.stack(
            [
                array.reshape(rows, splits, local, GROUP * HEAD_SIZE)[:, :, j].swapaxes(0, 1)
                for array in (query, d_out)
            ],
            axis=1,
        )
        for j in range(local)
    ]
    *both, parts = fence((*both, parts))

    blocks = [jnp.stack(parts)]
    for _ in range(1, WINDOW):
        blocks.append(shift(blocks[-1], "ctx", 1))
    chunks = []
    for j in range(local):
        if j > 0:
            both[j], chunks[j - 1], blocks = fence((both[j], chunks[j - 1], blocks))
        chunks.append(swap(both[j]))

    def home(dkv):
        return [dkv[0]] + [shift(dkv[t], "ctx", -t) for t in range(1, WINDOW)]

    def add(dkv):
        return sum(d.astype(WIDE) for d in dkv).astype(LOW)

    dq, dkv = [], []
    for j in range(local):
        dq_j, dkv_j = attention(ids, chunks[j], blocks, j)
        if j + 1 < local:
            dq_j, chunks[j + 1] = fence((dq_j, chunks[j + 1]))
        if j > 0:
            dq_j, dkv_j, dq[j - 1], dkv[j - 1] = fence((dq_j, dkv_j, dq[j - 1], dkv[j - 1]))
        dq.append(swap(dq_j))
        dkv.append(home(dkv_j))

    dkv = jnp.stack([add(d) for d in dkv], axis=1)
    dkv, dq[-1] = fence((dkv, dq[-1]))
    dkv = exchange(list(dkv), -1)
    dq = in_columns(
        dq, z, lambda z, j, part: [(part[g], 0, g * local + j) for g in range(splits)], 1
    )
    dq, dkv = fence((dq, dkv))
    dk, dv = in_columns(
        dkv,
        z,
        lambda z, s, part: [
            (
                part[j, :, i * HEAD_SIZE : (i + 1) * HEAD_SIZE],
                i,
                lax.rem(z + s, splits) * local + j,
            )
            for j in range(local)
            for i in range(2)
        ],
        2,
    )
    return dq[0], dk, dv


def solution(mesh):
    spec = P(("ctx", "head"), None)
    return jax.shard_map(
        body,
        mesh=mesh,
        in_specs=(spec, spec, spec, spec, P()),
        out_specs=(spec, spec, spec),
        check_vma=False,
    )
```

```python
import jax
import jax.numpy as jnp
from jax import lax
from jax.experimental import pallas as pl
from jax.experimental.pallas import tpu as pltpu
from jax.sharding import PartitionSpec as P

QUERY_HEAD_COUNT = 32
KEY_VALUE_HEADS = 8
GROUP = QUERY_HEAD_COUNT // KEY_VALUE_HEADS
HEAD_SIZE = 128
WINDOW = 4
TILES = 3 + 2 * (WINDOW - 1)
SCALE = HEAD_SIZE ** (-0.5)
LOG2_E = 1.4426950408889634
NT = (((1,), (1,)), ((), ()))
NN = (((1,), (0,)), ((), ()))
TN = (((0,), (0,)), ((), ()))
LOW = jnp.bfloat16
WIDE = jnp.float32
VMEM_LIMIT = 60 * 1024 * 1024
SCORE_BYTES = 24 * 1024 * 1024


def dot(a, b, dims):
    return lax.dot_general(a, b, dims, preferred_element_type=WIDE)


def fold(x, op):
    return op(x.reshape(x.shape[0] // 8, 8, x.shape[1]), axis=0)


def list_tiles(ids_ref, tile_ref):
    def slots(turn):
        first, second = ids_ref[2 * turn], ids_ref[2 * turn + 1]
        return jnp.where(first < second, 0, 1), jnp.minimum(first, second)

    def put(i, query_slot, turn, key_slot):
        tile_ref[3 * i] = query_slot
        tile_ref[3 * i + 1] = turn
        tile_ref[3 * i + 2] = key_slot

    low, stretch = slots(0)
    put(0, 0, 0, 0)
    put(1, 1, 0, 1)
    put(2, 1 - low, 0, low)
    for turn in range(1, WINDOW):
        key_low, key_stretch = slots(turn)
        later = stretch > key_stretch
        put(2 * turn + 1, 1 - low, turn, key_low)
        put(
            2 * turn + 2,
            jnp.where(later, low, 1 - low),
            turn,
            jnp.where(later, key_low, 1 - key_low),
        )


def attention_kernel(splits, heads, rows, at_once, head, came_apart, go_apart, ids_ref, *refs):
    parts_in, parts_out = splits if came_apart else 1, splits if go_apart else 1
    chunk_refs, block_refs = refs[:parts_in], refs[parts_in : parts_in + WINDOW]
    refs = refs[parts_in + WINDOW :]
    dq_outs, dkv_outs = refs[:parts_out], refs[parts_out : parts_out + WINDOW]
    (
        tile_ref, x_ref, kv_ref, qs_ref, gs_ref, st_ref, dp_ref, dqt_ref, dkv_ref,
        top_ref, total_ref, delta_ref, sem_ref,
    ) = refs[parts_out + WINDOW :]
    half = splits // 2
    stretch = half * rows
    width = at_once * stretch
    z = ids_ref[2 * WINDOW]
    step = pl.program_id(0) if heads > at_once else 0

    def place(block):
        return lax.rem(z - block + splits, splits)

    def lanes(h):
        return pl.ds(pl.multiple_of((step * at_once + h) * HEAD_SIZE, HEAD_SIZE), HEAD_SIZE)

    @pl.when(pl.program_id(0) == 0)
    def _():
        copies = [
            pltpu.make_async_copy(
                chunk_refs[s] if came_apart else chunk_refs[0].at[s], x_ref.at[s], sem_ref.at[s]
            )
            for s in range(splits)
        ]
        copies += [
            pltpu.make_async_copy(
                block.at[:, :, pl.ds(2 * head * HEAD_SIZE, 2 * HEAD_SIZE)],
                kv_ref.at[t],
                sem_ref.at[splits + t],
            )
            for t, block in enumerate(block_refs)
        ]
        for copy in copies:
            copy.start()
        list_tiles(ids_ref, tile_ref)
        dkv_ref[...] = jnp.zeros_like(dkv_ref)
        for copy in copies:
            copy.wait()

    for slot in range(2):
        for j in range(half):
            for h in range(at_once):
                at = pl.ds(h * stretch + j * rows, rows)
                block = slot * half + j
                s = place(block) if came_apart else block
                qs_ref[slot, at] = x_ref[s, 0, :, lanes(h)]
                gs_ref[slot, at] = x_ref[s, 1, :, lanes(h)]

    def part(which):
        return pl.ds(which * HEAD_SIZE, HEAD_SIZE)

    def tile(i):
        return tile_ref[3 * i], tile_ref[3 * i + 1], tile_ref[3 * i + 2]

    def keys(which, turn, key_slot):
        return jnp.concatenate(
            [kv_ref[turn, place(key_slot * half + j), :, part(which)] for j in range(half)], axis=0
        )

    def add_keys(which, turn, key_slot, update):
        for j in range(half):
            at = place(key_slot * half + j)
            dkv_ref[turn, at, :, part(which)] += update[j * rows : (j + 1) * rows]

    key_pos = lax.broadcasted_iota(jnp.int32, (stretch, width), 0)
    row_pos = lax.rem(lax.broadcasted_iota(jnp.int32, (stretch, width), 1), stretch)
    for slot in range(2):
        s = jnp.where(key_pos <= row_pos, dot(keys(0, 0, slot), qs_ref[slot], NT), -1e30)
        st_ref[slot] = s
        top_ref[slot] = fold(s, jnp.max)

    def scores(i, carry):
        slot, turn, key_slot = tile(i)
        s = dot(keys(0, turn, key_slot), qs_ref[slot], NT)
        st_ref[i] = s
        top_ref[slot] = jnp.maximum(top_ref[slot], fold(s, jnp.max))
        return carry

    lax.fori_loop(2, TILES, scores, 0, unroll=TILES - 2)
    top_ref[...] = jnp.broadcast_to(
        jnp.max(top_ref[...], axis=1, keepdims=True) * (SCALE * LOG2_E), top_ref.shape
    )
    total_ref[...] = jnp.zeros_like(total_ref)
    delta_ref[...] = jnp.zeros_like(delta_ref)
    dqt_ref[...] = jnp.zeros_like(dqt_ref)

    def weights(i, carry):
        slot, turn, key_slot = tile(i)
        p = jnp.exp2(st_ref[i] * (SCALE * LOG2_E) - top_ref[slot, 0:1])
        st_ref[i] = p
        total_ref[slot] += fold(p, jnp.sum)
        dp = dot(keys(1, turn, key_slot), gs_ref[slot], NT)
        dp_ref[i] = dp
        delta_ref[slot] += fold(p * dp, jnp.sum)
        return carry

    lax.fori_loop(0, TILES, weights, 0, unroll=3)
    total_ref[...] = jnp.broadcast_to(
        1.0 / jnp.sum(total_ref[...], axis=1, keepdims=True), total_ref.shape
    )
    delta_ref[...] = jnp.broadcast_to(
        jnp.sum(delta_ref[...], axis=1, keepdims=True) * total_ref[...], delta_ref.shape
    )

    def grads(i, carry):
        slot, turn, key_slot = tile(i)
        p = st_ref[i] * total_ref[slot, 0:1]
        ds = (p * (dp_ref[i] - delta_ref[slot, 0:1])).astype(LOW)
        add_keys(1, turn, key_slot, dot(p.astype(LOW), gs_ref[slot], NN))
        add_keys(0, turn, key_slot, dot(ds, qs_ref[slot], NN))
        dqt_ref[slot] += dot(keys(0, turn, key_slot), ds, TN)
        return carry

    lax.fori_loop(0, TILES, grads, 0, unroll=TILES)

    for slot in range(2):
        dq = (dqt_ref[slot] * SCALE).T.astype(LOW)
        for j in range(half):
            for h in range(at_once):
                at = h * stretch + j * rows
                block = slot * half + j
                s = place(block) if go_apart else block
                x_ref[s, 0, :, lanes(h)] = dq[at : at + rows]

    @pl.when(pl.program_id(0) == heads // at_once - 1)
    def _():
        for s in range(splits):
            if go_apart:
                dq_outs[s][...] = x_ref[s, 0]
            else:
                dq_outs[0][s] = x_ref[s, 0]
        for t, out in enumerate(dkv_outs):
            out[:, :, part(0)] = (dkv_ref[t, :, :, part(0)] * SCALE).astype(LOW)
            out[:, :, part(1)] = dkv_ref[t, :, :, part(1)].astype(LOW)


def attention(ids, chunk, blocks, head, go_apart):
    came_apart = isinstance(chunk, list)
    splits = len(chunk)
    _, rows, lanes = chunk[0].shape
    heads = lanes // HEAD_SIZE
    stretch = splits // 2 * rows
    at_once = heads
    while 2 * TILES * 4 * stretch * stretch * at_once > SCORE_BYTES and at_once % 2 == 0:
        at_once //= 2
    width = at_once * stretch

    def kernel(*refs):
        attention_kernel(splits, heads, rows, at_once, head, came_apart, go_apart, *refs)

    def whole(shape):
        return pl.BlockSpec(shape, lambda i: (0,) * len(shape), pipeline_mode=pl.Buffered(1))

    chunk = chunk if came_apart else [chunk]
    dq_shapes = [(rows, lanes)] * splits if go_apart else [(splits, rows, lanes)]
    dkv_shape = (splits, rows, 2 * HEAD_SIZE)
    out = pl.pallas_call(
        kernel,
        grid=(heads // at_once,),
        in_specs=[pl.BlockSpec(memory_space=pltpu.SMEM)]
        + [pl.BlockSpec(memory_space=pl.ANY)] * (len(chunk) + WINDOW),
        out_specs=[whole(shape) for shape in dq_shapes] + [whole(dkv_shape)] * WINDOW,
        out_shape=[jax.ShapeDtypeStruct(shape, LOW) for shape in dq_shapes]
        + [jax.ShapeDtypeStruct(dkv_shape, LOW)] * WINDOW,
        scratch_shapes=[
            pltpu.SMEM((3 * TILES,), jnp.int32),
            pltpu.VMEM((splits, 2, rows, lanes), LOW),
            pltpu.VMEM((WINDOW, splits, rows, 2 * HEAD_SIZE), LOW),
            pltpu.VMEM((2, width, HEAD_SIZE), LOW),
            pltpu.VMEM((2, width, HEAD_SIZE), LOW),
            pltpu.VMEM((TILES, stretch, width), WIDE),
            pltpu.VMEM((TILES, stretch, width), WIDE),
            pltpu.VMEM((2, HEAD_SIZE, width), WIDE),
            pltpu.VMEM((WINDOW, splits, rows, 2 * HEAD_SIZE), WIDE),
            pltpu.VMEM((2, 8, width), WIDE),
            pltpu.VMEM((2, 8, width), WIDE),
            pltpu.VMEM((2, 8, width), WIDE),
            pltpu.SemaphoreType.DMA((splits + WINDOW,)),
        ],
        compiler_params=pltpu.CompilerParams(vmem_limit_bytes=VMEM_LIMIT),
        cost_estimate=pl.CostEstimate(
            flops=16 * 2 * 5 * TILES * stretch * stretch * heads * HEAD_SIZE // 4,
            bytes_accessed=1 << 22,
            transcendentals=0,
        ),
    )(ids, *chunk, *blocks)
    return out[:splits] if go_apart else out[0], out[-WINDOW:]


def in_columns(parts, z, places, outs):
    rows = parts[0].shape[-2]

    def kernel(z_ref, *refs):
        part_refs, out_refs = refs[: len(parts)], refs[len(parts) :]
        for index, part in enumerate(part_refs):
            for piece, out, column in places(z_ref[0], index, part):
                width = piece.shape[-1]
                start = pl.multiple_of(column * width, HEAD_SIZE)
                out_refs[out][:, pl.ds(start, width)] = piece

    size = sum(part.size for part in parts) // rows // outs
    return pl.pallas_call(
        kernel,
        in_specs=[pl.BlockSpec(memory_space=pltpu.SMEM)]
        + [pl.BlockSpec(memory_space=pltpu.VMEM)] * len(parts),
        out_specs=[pl.BlockSpec(memory_space=pltpu.VMEM)] * outs,
        out_shape=[jax.ShapeDtypeStruct((rows, size), LOW)] * outs,
        compiler_params=pltpu.CompilerParams(vmem_limit_bytes=VMEM_LIMIT),
    )(z.astype(jnp.int32)[None], *parts)


def body(query, key, value, d_out, stretch_ids):
    rows = query.shape[0]
    ranks = lax.axis_size("ctx")
    splits = lax.axis_size("head")
    local = KEY_VALUE_HEADS // splits
    z = lax.axis_index("head")
    rank = lax.axis_index("ctx")
    fence = lax.optimization_barrier

    def shift(array, axis, by):
        size = lax.axis_size(axis)
        return lax.ppermute(array, axis, [(i, (i + by) % size) for i in range(size)])

    def exchange(chunks, sign):
        return [chunks[0]] + [shift(chunks[s], "head", sign * s) for s in range(1, splits)]

    def swap(array):
        return lax.all_to_all(array, "head", split_axis=0, concat_axis=0, tiled=True)

    def ids_of(turn):
        source = lax.rem(rank - turn + ranks, ranks)
        return lax.dynamic_slice_in_dim(stretch_ids, 2 * source, 2)

    ids = jnp.concatenate([ids_of(t) for t in range(WINDOW)] + [z.astype(jnp.int32)[None]])

    def for_device_ahead(s):
        start = lax.rem(z + s, splits) * (local * HEAD_SIZE)
        ahead = [
            lax.dynamic_slice_in_dim(array, start, local * HEAD_SIZE, 1) for array in (key, value)
        ]
        return jnp.concatenate(
            [
                array[:, j * HEAD_SIZE : (j + 1) * HEAD_SIZE]
                for j in range(local)
                for array in ahead
            ],
            axis=1,
        )

    parts = exchange([for_device_ahead(s) for s in range(splits)], 1)
    def in_order(j):
        split = [
            array.reshape(rows, splits, local, GROUP * HEAD_SIZE)[:, :, j].swapaxes(0, 1)
            for array in (query, d_out)
        ]
        return jnp.stack(split, axis=1)

    def apart(j):
        start = [(lax.rem(z + s, splits) * local + j) * GROUP * HEAD_SIZE for s in range(splits)]
        return [
            jnp.stack(
                [
                    lax.dynamic_slice_in_dim(array, at, GROUP * HEAD_SIZE, 1)
                    for array in (query, d_out)
                ]
            )
            for at in start
        ]

    both = [in_order(0)] + [apart(j) for j in range(1, local)]
    *both, parts = fence((*both, parts))

    blocks = [jnp.stack(parts)]
    for _ in range(1, WINDOW):
        blocks.append(shift(blocks[-1], "ctx", 1))
    chunks = [swap(both[0])]
    for j in range(1, local):
        both[j], chunks[j - 1] = fence((both[j], chunks[j - 1]))
        chunks.append(exchange(both[j], 1))

    def home(dkv):
        return [dkv[0]] + [shift(dkv[t], "ctx", -t) for t in range(1, WINDOW)]

    def add(dkv):
        return sum(d.astype(WIDE) for d in dkv).astype(LOW)

    dq, dkv = [], []
    for j in range(local):
        last = j > 0 and j == local - 1
        dq_j, dkv_j = attention(ids, chunks[j], blocks, j, last)
        if j > 0:
            dkv_j, dkv[j - 1] = fence((dkv_j, dkv[j - 1]))
            dq_j, dq[j - 1] = fence((dq_j, dq[j - 1]))
        dq.append(exchange(dq_j, -1) if last else swap(dq_j))
        dkv.append(home(dkv_j))

    dkv = jnp.stack([add(d) for d in dkv], axis=1)
    dkv, dq[-1] = fence((dkv, dq[-1]))
    dkv = exchange(list(dkv), -1)
    columns, pieces = [], []
    for j, part in enumerate(dq):
        if isinstance(part, list):
            columns += [[(s, j, None)] for s in range(splits)]
            pieces += part
        else:
            columns.append([(g, j, g) for g in range(splits)])
            pieces.append(part)
    dq = in_columns(
        pieces,
        z,
        lambda z, index, part: [
            (part[...], 0, lax.rem(z + s, splits) * local + j)
            if g is None
            else (part[g], 0, g * local + j)
            for s, j, g in columns[index]
        ],
        1,
    )
    dq, dkv = fence((dq, dkv))
    dk, dv = in_columns(
        dkv,
        z,
        lambda z, s, part: [
            (
                part[j, :, i * HEAD_SIZE : (i + 1) * HEAD_SIZE],
                i,
                lax.rem(z + s, splits) * local + j,
            )
            for j in range(local)
            for i in range(2)
        ],
        2,
    )
    return dq[0], dk, dv


def solution(mesh):
    spec = P(("ctx", "head"), None)
    return jax.shard_map(
        body,
        mesh=mesh,
        in_specs=(spec, spec, spec, spec, P()),
        out_specs=(spec, spec, spec),
        check_vma=False,
    )
```

```python
import jax
import jax.numpy as jnp
from jax import lax
from jax.experimental import pallas as pl
from jax.experimental.pallas import tpu as pltpu
from jax.sharding import PartitionSpec as P

QUERY_HEAD_COUNT = 32
KEY_VALUE_HEADS = 8
GROUP = QUERY_HEAD_COUNT // KEY_VALUE_HEADS
HEAD_SIZE = 128
WINDOW = 4
TILES = 3 + 2 * (WINDOW - 1)
SCALE = HEAD_SIZE ** (-0.5)
LOG2_E = 1.4426950408889634
NT = (((1,), (1,)), ((), ()))
NN = (((1,), (0,)), ((), ()))
TN = (((0,), (0,)), ((), ()))
LOW = jnp.bfloat16
WIDE = jnp.float32
VMEM_LIMIT = 60 * 1024 * 1024
SCORE_BYTES = 24 * 1024 * 1024


def dot(a, b, dims):
    return lax.dot_general(a, b, dims, preferred_element_type=WIDE)


def fold(x, op):
    return op(x.reshape(x.shape[0] // 8, 8, x.shape[1]), axis=0)


def list_tiles(ids_ref, tile_ref):
    def slots(turn):
        first, second = ids_ref[2 * turn], ids_ref[2 * turn + 1]
        return jnp.where(first < second, 0, 1), jnp.minimum(first, second)

    def put(i, query_slot, turn, key_slot):
        tile_ref[3 * i] = query_slot
        tile_ref[3 * i + 1] = turn
        tile_ref[3 * i + 2] = key_slot

    low, stretch = slots(0)
    put(0, 0, 0, 0)
    put(1, 1, 0, 1)
    put(2, 1 - low, 0, low)
    for turn in range(1, WINDOW):
        key_low, key_stretch = slots(turn)
        later = stretch > key_stretch
        put(2 * turn + 1, 1 - low, turn, key_low)
        put(
            2 * turn + 2,
            jnp.where(later, low, 1 - low),
            turn,
            jnp.where(later, key_low, 1 - key_low),
        )


def attention_kernel(splits, heads, rows, at_once, head, came_apart, go_apart, ids_ref, *refs):
    parts_in, parts_out = splits if came_apart else 1, splits if go_apart else 1
    chunk_refs, block_refs = refs[:parts_in], refs[parts_in : parts_in + WINDOW]
    refs = refs[parts_in + WINDOW :]
    dq_outs, dkv_outs = refs[:parts_out], refs[parts_out : parts_out + WINDOW]
    (
        tile_ref, x_ref, kv_ref, qs_ref, gs_ref, st_ref, dp_ref, dqt_ref, dkv_ref,
        top_ref, total_ref, delta_ref, sem_ref,
    ) = refs[parts_out + WINDOW :]
    half = splits // 2
    stretch = half * rows
    width = at_once * stretch
    z = ids_ref[2 * WINDOW]
    step = pl.program_id(0) if heads > at_once else 0

    def place(block):
        return lax.rem(z - block + splits, splits)

    def lanes(h):
        return pl.ds(pl.multiple_of((step * at_once + h) * HEAD_SIZE, HEAD_SIZE), HEAD_SIZE)

    @pl.when(pl.program_id(0) == 0)
    def _():
        copies = [
            pltpu.make_async_copy(
                chunk_refs[s] if came_apart else chunk_refs[0].at[s], x_ref.at[s], sem_ref.at[s]
            )
            for s in range(splits)
        ]
        copies += [
            pltpu.make_async_copy(
                block.at[:, :, pl.ds(2 * head * HEAD_SIZE, 2 * HEAD_SIZE)],
                kv_ref.at[t],
                sem_ref.at[splits + t],
            )
            for t, block in enumerate(block_refs)
        ]
        for copy in copies:
            copy.start()
        list_tiles(ids_ref, tile_ref)
        dkv_ref[...] = jnp.zeros_like(dkv_ref)
        for copy in copies:
            copy.wait()

    for slot in range(2):
        for j in range(half):
            for h in range(at_once):
                at = pl.ds(h * stretch + j * rows, rows)
                block = slot * half + j
                s = place(block) if came_apart else block
                qs_ref[slot, at] = x_ref[s, 0, :, lanes(h)]
                gs_ref[slot, at] = x_ref[s, 1, :, lanes(h)]

    def part(which):
        return pl.ds(which * HEAD_SIZE, HEAD_SIZE)

    def tile(i):
        return tile_ref[3 * i], tile_ref[3 * i + 1], tile_ref[3 * i + 2]

    def keys(which, turn, key_slot):
        return jnp.concatenate(
            [kv_ref[turn, place(key_slot * half + j), :, part(which)] for j in range(half)], axis=0
        )

    def add_keys(which, turn, key_slot, update):
        for j in range(half):
            at = place(key_slot * half + j)
            dkv_ref[turn, at, :, part(which)] += update[j * rows : (j + 1) * rows]

    key_pos = lax.broadcasted_iota(jnp.int32, (stretch, width), 0)
    row_pos = lax.rem(lax.broadcasted_iota(jnp.int32, (stretch, width), 1), stretch)
    for slot in range(2):
        s = jnp.where(key_pos <= row_pos, dot(keys(0, 0, slot), qs_ref[slot], NT), -1e30)
        st_ref[slot] = s
        top_ref[slot] = fold(s, jnp.max)

    def scores(i, carry):
        slot, turn, key_slot = tile(i)
        s = dot(keys(0, turn, key_slot), qs_ref[slot], NT)
        st_ref[i] = s
        top_ref[slot] = jnp.maximum(top_ref[slot], fold(s, jnp.max))
        return carry

    lax.fori_loop(2, TILES, scores, 0, unroll=TILES - 2)
    top_ref[...] = jnp.broadcast_to(
        jnp.max(top_ref[...], axis=1, keepdims=True) * (SCALE * LOG2_E), top_ref.shape
    )
    total_ref[...] = jnp.zeros_like(total_ref)
    delta_ref[...] = jnp.zeros_like(delta_ref)
    dqt_ref[...] = jnp.zeros_like(dqt_ref)

    def weights(i, carry):
        slot, turn, key_slot = tile(i)
        p = jnp.exp2(st_ref[i] * (SCALE * LOG2_E) - top_ref[slot, 0:1])
        st_ref[i] = p
        total_ref[slot] += fold(p, jnp.sum)
        dp = dot(keys(1, turn, key_slot), gs_ref[slot], NT)
        dp_ref[i] = dp
        delta_ref[slot] += fold(p * dp, jnp.sum)
        return carry

    lax.fori_loop(0, TILES, weights, 0, unroll=3)
    total_ref[...] = jnp.broadcast_to(
        1.0 / jnp.sum(total_ref[...], axis=1, keepdims=True), total_ref.shape
    )
    delta_ref[...] = jnp.broadcast_to(
        jnp.sum(delta_ref[...], axis=1, keepdims=True) * total_ref[...], delta_ref.shape
    )

    def grads(i, carry):
        slot, turn, key_slot = tile(i)
        p = st_ref[i] * total_ref[slot, 0:1]
        ds = (p * (dp_ref[i] - delta_ref[slot, 0:1])).astype(LOW)
        add_keys(1, turn, key_slot, dot(p.astype(LOW), gs_ref[slot], NN))
        add_keys(0, turn, key_slot, dot(ds, qs_ref[slot], NN))
        dqt_ref[slot] += dot(keys(0, turn, key_slot), ds, TN)
        return carry

    lax.fori_loop(0, TILES, grads, 0, unroll=TILES)

    for slot in range(2):
        dq = (dqt_ref[slot] * SCALE).T.astype(LOW)
        for j in range(half):
            for h in range(at_once):
                at = h * stretch + j * rows
                block = slot * half + j
                s = place(block) if go_apart else block
                x_ref[s, 0, :, lanes(h)] = dq[at : at + rows]

    @pl.when(pl.program_id(0) == heads // at_once - 1)
    def _():
        for s in range(splits):
            if go_apart:
                dq_outs[s][...] = x_ref[s, 0]
            else:
                dq_outs[0][s] = x_ref[s, 0]
        for t, out in enumerate(dkv_outs):
            out[:, :, part(0)] = (dkv_ref[t, :, :, part(0)] * SCALE).astype(LOW)
            out[:, :, part(1)] = dkv_ref[t, :, :, part(1)].astype(LOW)


def attention(ids, chunk, blocks, head, go_apart):
    came_apart = isinstance(chunk, list)
    splits = len(chunk)
    _, rows, lanes = chunk[0].shape
    heads = lanes // HEAD_SIZE
    stretch = splits // 2 * rows
    at_once = heads
    while 2 * TILES * 4 * stretch * stretch * at_once > SCORE_BYTES and at_once % 2 == 0:
        at_once //= 2
    width = at_once * stretch

    def kernel(*refs):
        attention_kernel(splits, heads, rows, at_once, head, came_apart, go_apart, *refs)

    def whole(shape):
        return pl.BlockSpec(shape, lambda i: (0,) * len(shape), pipeline_mode=pl.Buffered(1))

    chunk = chunk if came_apart else [chunk]
    dq_shapes = [(rows, lanes)] * splits if go_apart else [(splits, rows, lanes)]
    dkv_shape = (splits, rows, 2 * HEAD_SIZE)
    out = pl.pallas_call(
        kernel,
        grid=(heads // at_once,),
        in_specs=[pl.BlockSpec(memory_space=pltpu.SMEM)]
        + [pl.BlockSpec(memory_space=pl.ANY)] * (len(chunk) + WINDOW),
        out_specs=[whole(shape) for shape in dq_shapes] + [whole(dkv_shape)] * WINDOW,
        out_shape=[jax.ShapeDtypeStruct(shape, LOW) for shape in dq_shapes]
        + [jax.ShapeDtypeStruct(dkv_shape, LOW)] * WINDOW,
        scratch_shapes=[
            pltpu.SMEM((3 * TILES,), jnp.int32),
            pltpu.VMEM((splits, 2, rows, lanes), LOW),
            pltpu.VMEM((WINDOW, splits, rows, 2 * HEAD_SIZE), LOW),
            pltpu.VMEM((2, width, HEAD_SIZE), LOW),
            pltpu.VMEM((2, width, HEAD_SIZE), LOW),
            pltpu.VMEM((TILES, stretch, width), WIDE),
            pltpu.VMEM((TILES, stretch, width), WIDE),
            pltpu.VMEM((2, HEAD_SIZE, width), WIDE),
            pltpu.VMEM((WINDOW, splits, rows, 2 * HEAD_SIZE), WIDE),
            pltpu.VMEM((2, 8, width), WIDE),
            pltpu.VMEM((2, 8, width), WIDE),
            pltpu.VMEM((2, 8, width), WIDE),
            pltpu.SemaphoreType.DMA((splits + WINDOW,)),
        ],
        compiler_params=pltpu.CompilerParams(vmem_limit_bytes=VMEM_LIMIT),
        cost_estimate=pl.CostEstimate(
            flops=16 * 2 * 5 * TILES * stretch * stretch * heads * HEAD_SIZE // 4,
            bytes_accessed=1 << 22,
            transcendentals=0,
        ),
    )(ids, *chunk, *blocks)
    return out[:splits] if go_apart else out[0], out[-WINDOW:]


def in_columns(parts, z, places, outs):
    rows = parts[0].shape[-2]

    def kernel(z_ref, *refs):
        part_refs, out_refs = refs[: len(parts)], refs[len(parts) :]
        for index, part in enumerate(part_refs):
            for piece, out, column in places(z_ref[0], index, part):
                width = piece.shape[-1]
                start = pl.multiple_of(column * width, HEAD_SIZE)
                out_refs[out][:, pl.ds(start, width)] = piece

    size = sum(part.size for part in parts) // rows // outs
    return pl.pallas_call(
        kernel,
        in_specs=[pl.BlockSpec(memory_space=pltpu.SMEM)]
        + [pl.BlockSpec(memory_space=pltpu.VMEM)] * len(parts),
        out_specs=[pl.BlockSpec(memory_space=pltpu.VMEM)] * outs,
        out_shape=[jax.ShapeDtypeStruct((rows, size), LOW)] * outs,
        compiler_params=pltpu.CompilerParams(vmem_limit_bytes=8 * 1024 * 1024),
    )(z.astype(jnp.int32)[None], *parts)


def body(query, key, value, d_out, stretch_ids):
    rows = query.shape[0]
    ranks = lax.axis_size("ctx")
    splits = lax.axis_size("head")
    local = KEY_VALUE_HEADS // splits
    z = lax.axis_index("head")
    rank = lax.axis_index("ctx")
    fence = lax.optimization_barrier

    def shift(array, axis, by):
        size = lax.axis_size(axis)
        return lax.ppermute(array, axis, [(i, (i + by) % size) for i in range(size)])

    def exchange(chunks, sign):
        return [chunks[0]] + [shift(chunks[s], "head", sign * s) for s in range(1, splits)]

    def swap(array):
        return lax.all_to_all(array, "head", split_axis=0, concat_axis=0, tiled=True)

    def ids_of(turn):
        source = lax.rem(rank - turn + ranks, ranks)
        return lax.dynamic_slice_in_dim(stretch_ids, 2 * source, 2)

    ids = jnp.concatenate([ids_of(t) for t in range(WINDOW)] + [z.astype(jnp.int32)[None]])

    def for_device_ahead(s):
        start = lax.rem(z + s, splits) * (local * HEAD_SIZE)
        ahead = [
            lax.dynamic_slice_in_dim(array, start, local * HEAD_SIZE, 1) for array in (key, value)
        ]
        return jnp.concatenate(
            [
                array[:, j * HEAD_SIZE : (j + 1) * HEAD_SIZE]
                for j in range(local)
                for array in ahead
            ],
            axis=1,
        )

    parts = exchange([for_device_ahead(s) for s in range(splits)], 1)
    def in_order(j):
        split = [
            array.reshape(rows, splits, local, GROUP * HEAD_SIZE)[:, :, j].swapaxes(0, 1)
            for array in (query, d_out)
        ]
        return jnp.stack(split, axis=1)

    def apart(j):
        start = [(lax.rem(z + s, splits) * local + j) * GROUP * HEAD_SIZE for s in range(splits)]
        return [
            jnp.stack(
                [
                    lax.dynamic_slice_in_dim(array, at, GROUP * HEAD_SIZE, 1)
                    for array in (query, d_out)
                ]
            )
            for at in start
        ]

    both = [in_order(0)] + [apart(j) for j in range(1, local)]
    *both, parts = fence((*both, parts))

    blocks = [jnp.stack(parts)]
    for _ in range(1, WINDOW):
        blocks.append(shift(blocks[-1], "ctx", 1))
    chunks = [swap(both[0])]
    for j in range(1, local):
        both[j], chunks[j - 1] = fence((both[j], chunks[j - 1]))
        chunks.append(exchange(both[j], 1))

    def home(dkv):
        return [dkv[0]] + [shift(dkv[t], "ctx", -t) for t in range(1, WINDOW)]

    def add(dkv):
        return sum(d.astype(WIDE) for d in dkv).astype(LOW)

    near = [s for s in range(1, splits) if 2 * s != splits]
    dq, dkv = [], []
    for j in range(local):
        last = j > 0 and j == local - 1
        dq_j, dkv_j = attention(ids, chunks[j], blocks, j, last)
        if j + 1 < local:
            came = chunks[j + 1]
            came = [came[s] for s in near]
            dq_j, came = fence((dq_j, came))
            for s, part in zip(near, came):
                chunks[j + 1][s] = part
        if j > 0:
            dkv_j, dkv[j - 1] = fence((dkv_j, dkv[j - 1]))
            dq_j, dq[j - 1] = fence((dq_j, dq[j - 1]))
        dq.append(exchange(dq_j, -1) if last else swap(dq_j))
        dkv.append(home(dkv_j))

    dkv = jnp.stack([add(d) for d in dkv], axis=1)
    dkv, dq[-1] = fence((dkv, dq[-1]))
    dkv = exchange(list(dkv), -1)
    columns, pieces = [], []
    for j, part in enumerate(dq):
        if isinstance(part, list):
            columns += [[(s, j, None)] for s in range(splits)]
            pieces += part
        else:
            columns.append([(g, j, g) for g in range(splits)])
            pieces.append(part)
    dq = in_columns(
        pieces,
        z,
        lambda z, index, part: [
            (part[...], 0, lax.rem(z + s, splits) * local + j)
            if g is None
            else (part[g], 0, g * local + j)
            for s, j, g in columns[index]
        ],
        1,
    )
    dq, dkv = fence((dq, dkv))
    dk, dv = in_columns(
        dkv,
        z,
        lambda z, s, part: [
            (
                part[j, :, i * HEAD_SIZE : (i + 1) * HEAD_SIZE],
                i,
                lax.rem(z + s, splits) * local + j,
            )
            for j in range(local)
            for i in range(2)
        ],
        2,
    )
    return dq[0], dk, dv


def solution(mesh):
    spec = P(("ctx", "head"), None)
    return jax.shard_map(
        body,
        mesh=mesh,
        in_specs=(spec, spec, spec, spec, P()),
        out_specs=(spec, spec, spec),
        check_vma=False,
    )
```

```python
import jax
import jax.numpy as jnp
from jax import lax
from jax.experimental import pallas as pl
from jax.experimental.pallas import tpu as pltpu
from jax.sharding import PartitionSpec as P

QUERY_HEAD_COUNT = 32
KEY_VALUE_HEADS = 8
GROUP = QUERY_HEAD_COUNT // KEY_VALUE_HEADS
HEAD_SIZE = 128
WINDOW = 4
TILES = 3 + 2 * (WINDOW - 1)
SCALE = HEAD_SIZE ** (-0.5)
LOG2_E = 1.4426950408889634
NT = (((1,), (1,)), ((), ()))
NN = (((1,), (0,)), ((), ()))
TN = (((0,), (0,)), ((), ()))
LOW = jnp.bfloat16
WIDE = jnp.float32
VMEM_LIMIT = 60 * 1024 * 1024
SCORE_BYTES = 24 * 1024 * 1024


def dot(a, b, dims):
    return lax.dot_general(a, b, dims, preferred_element_type=WIDE)


def fold(x, op):
    return op(x.reshape(x.shape[0] // 8, 8, x.shape[1]), axis=0)


def list_tiles(ids_ref, tile_ref):
    def slots(turn):
        first, second = ids_ref[2 * turn], ids_ref[2 * turn + 1]
        return jnp.where(first < second, 0, 1), jnp.minimum(first, second)

    def put(i, query_slot, turn, key_slot):
        tile_ref[3 * i] = query_slot
        tile_ref[3 * i + 1] = turn
        tile_ref[3 * i + 2] = key_slot

    low, stretch = slots(0)
    put(0, 0, 0, 0)
    put(1, 1, 0, 1)
    put(2, 1 - low, 0, low)
    for turn in range(1, WINDOW):
        key_low, key_stretch = slots(turn)
        later = stretch > key_stretch
        put(2 * turn + 1, 1 - low, turn, key_low)
        put(
            2 * turn + 2,
            jnp.where(later, low, 1 - low),
            turn,
            jnp.where(later, key_low, 1 - key_low),
        )


def attention_kernel(splits, heads, rows, at_once, head, came_apart, go_apart, ids_ref, *refs):
    parts_in, parts_out = splits if came_apart else 1, splits if go_apart else 1
    chunk_refs, block_refs = refs[:parts_in], refs[parts_in : parts_in + WINDOW]
    refs = refs[parts_in + WINDOW :]
    dq_outs, dkv_outs = refs[:parts_out], refs[parts_out : parts_out + WINDOW]
    (
        tile_ref, x_ref, kv_ref, qs_ref, gs_ref, st_ref, dp_ref, dqt_ref, dkv_ref,
        top_ref, total_ref, delta_ref, sem_ref,
    ) = refs[parts_out + WINDOW :]
    half = splits // 2
    stretch = half * rows
    width = at_once * stretch
    z = ids_ref[2 * WINDOW]
    step = pl.program_id(0) if heads > at_once else 0

    def place(block):
        return lax.rem(z - block + splits, splits)

    def lanes(h):
        return pl.ds(pl.multiple_of((step * at_once + h) * HEAD_SIZE, HEAD_SIZE), HEAD_SIZE)

    @pl.when(pl.program_id(0) == 0)
    def _():
        copies = [
            pltpu.make_async_copy(
                chunk_refs[s] if came_apart else chunk_refs[0].at[s], x_ref.at[s], sem_ref.at[s]
            )
            for s in range(splits)
        ]
        copies += [
            pltpu.make_async_copy(
                block.at[:, :, pl.ds(2 * head * HEAD_SIZE, 2 * HEAD_SIZE)],
                kv_ref.at[t],
                sem_ref.at[splits + t],
            )
            for t, block in enumerate(block_refs)
        ]
        for copy in copies:
            copy.start()
        list_tiles(ids_ref, tile_ref)
        dkv_ref[...] = jnp.zeros_like(dkv_ref)
        for copy in copies:
            copy.wait()

    for slot in range(2):
        for j in range(half):
            for h in range(at_once):
                at = pl.ds(h * stretch + j * rows, rows)
                block = slot * half + j
                s = place(block) if came_apart else block
                qs_ref[slot, at] = x_ref[s, 0, :, lanes(h)]
                gs_ref[slot, at] = x_ref[s, 1, :, lanes(h)]

    def part(which):
        return pl.ds(which * HEAD_SIZE, HEAD_SIZE)

    def tile(i):
        return tile_ref[3 * i], tile_ref[3 * i + 1], tile_ref[3 * i + 2]

    def keys(which, turn, key_slot):
        return jnp.concatenate(
            [kv_ref[turn, place(key_slot * half + j), :, part(which)] for j in range(half)], axis=0
        )

    def add_keys(which, turn, key_slot, update):
        for j in range(half):
            at = place(key_slot * half + j)
            dkv_ref[turn, at, :, part(which)] += update[j * rows : (j + 1) * rows]

    key_pos = lax.broadcasted_iota(jnp.int32, (stretch, width), 0)
    row_pos = lax.rem(lax.broadcasted_iota(jnp.int32, (stretch, width), 1), stretch)
    for slot in range(2):
        s = jnp.where(key_pos <= row_pos, dot(keys(0, 0, slot), qs_ref[slot], NT), -1e30)
        st_ref[slot] = s
        top_ref[slot] = fold(s, jnp.max)

    def scores(i, carry):
        slot, turn, key_slot = tile(i)
        s = dot(keys(0, turn, key_slot), qs_ref[slot], NT)
        st_ref[i] = s
        top_ref[slot] = jnp.maximum(top_ref[slot], fold(s, jnp.max))
        return carry

    lax.fori_loop(2, TILES, scores, 0, unroll=TILES - 2)
    top_ref[...] = jnp.broadcast_to(
        jnp.max(top_ref[...], axis=1, keepdims=True) * (SCALE * LOG2_E), top_ref.shape
    )
    total_ref[...] = jnp.zeros_like(total_ref)
    delta_ref[...] = jnp.zeros_like(delta_ref)
    dqt_ref[...] = jnp.zeros_like(dqt_ref)

    def weights(i, carry):
        slot, turn, key_slot = tile(i)
        p = jnp.exp2(st_ref[i] * (SCALE * LOG2_E) - top_ref[slot, 0:1])
        st_ref[i] = p
        total_ref[slot] += fold(p, jnp.sum)
        dp = dot(keys(1, turn, key_slot), gs_ref[slot], NT)
        dp_ref[i] = dp
        delta_ref[slot] += fold(p * dp, jnp.sum)
        return carry

    lax.fori_loop(0, TILES, weights, 0, unroll=3)
    total_ref[...] = jnp.broadcast_to(
        1.0 / jnp.sum(total_ref[...], axis=1, keepdims=True), total_ref.shape
    )
    delta_ref[...] = jnp.broadcast_to(
        jnp.sum(delta_ref[...], axis=1, keepdims=True) * total_ref[...], delta_ref.shape
    )

    def grads(i, carry):
        slot, turn, key_slot = tile(i)
        p = st_ref[i] * total_ref[slot, 0:1]
        ds = (p * (dp_ref[i] - delta_ref[slot, 0:1])).astype(LOW)
        add_keys(1, turn, key_slot, dot(p.astype(LOW), gs_ref[slot], NN))
        add_keys(0, turn, key_slot, dot(ds, qs_ref[slot], NN))
        dqt_ref[slot] += dot(keys(0, turn, key_slot), ds, TN)
        return carry

    lax.fori_loop(0, TILES, grads, 0, unroll=TILES)

    for slot in range(2):
        dq = (dqt_ref[slot] * SCALE).T.astype(LOW)
        for j in range(half):
            for h in range(at_once):
                at = h * stretch + j * rows
                block = slot * half + j
                s = place(block) if go_apart else block
                x_ref[s, 0, :, lanes(h)] = dq[at : at + rows]

    @pl.when(pl.program_id(0) == heads // at_once - 1)
    def _():
        for s in range(splits):
            if go_apart:
                dq_outs[s][...] = x_ref[s, 0]
            else:
                dq_outs[0][s] = x_ref[s, 0]
        for t, out in enumerate(dkv_outs):
            out[:, :, part(0)] = (dkv_ref[t, :, :, part(0)] * SCALE).astype(LOW)
            out[:, :, part(1)] = dkv_ref[t, :, :, part(1)].astype(LOW)


def attention(ids, chunk, blocks, head, go_apart):
    came_apart = isinstance(chunk, list)
    splits = len(chunk)
    _, rows, lanes = chunk[0].shape
    heads = lanes // HEAD_SIZE
    stretch = splits // 2 * rows
    at_once = heads
    while 2 * TILES * 4 * stretch * stretch * at_once > SCORE_BYTES and at_once % 2 == 0:
        at_once //= 2
    width = at_once * stretch

    def kernel(*refs):
        attention_kernel(splits, heads, rows, at_once, head, came_apart, go_apart, *refs)

    def whole(shape):
        return pl.BlockSpec(shape, lambda i: (0,) * len(shape), pipeline_mode=pl.Buffered(1))

    chunk = chunk if came_apart else [chunk]
    dq_shapes = [(rows, lanes)] * splits if go_apart else [(splits, rows, lanes)]
    dkv_shape = (splits, rows, 2 * HEAD_SIZE)
    out = pl.pallas_call(
        kernel,
        grid=(heads // at_once,),
        in_specs=[pl.BlockSpec(memory_space=pltpu.SMEM)]
        + [pl.BlockSpec(memory_space=pl.ANY)] * (len(chunk) + WINDOW),
        out_specs=[whole(shape) for shape in dq_shapes] + [whole(dkv_shape)] * WINDOW,
        out_shape=[jax.ShapeDtypeStruct(shape, LOW) for shape in dq_shapes]
        + [jax.ShapeDtypeStruct(dkv_shape, LOW)] * WINDOW,
        scratch_shapes=[
            pltpu.SMEM((3 * TILES,), jnp.int32),
            pltpu.VMEM((splits, 2, rows, lanes), LOW),
            pltpu.VMEM((WINDOW, splits, rows, 2 * HEAD_SIZE), LOW),
            pltpu.VMEM((2, width, HEAD_SIZE), LOW),
            pltpu.VMEM((2, width, HEAD_SIZE), LOW),
            pltpu.VMEM((TILES, stretch, width), WIDE),
            pltpu.VMEM((TILES, stretch, width), WIDE),
            pltpu.VMEM((2, HEAD_SIZE, width), WIDE),
            pltpu.VMEM((WINDOW, splits, rows, 2 * HEAD_SIZE), WIDE),
            pltpu.VMEM((2, 8, width), WIDE),
            pltpu.VMEM((2, 8, width), WIDE),
            pltpu.VMEM((2, 8, width), WIDE),
            pltpu.SemaphoreType.DMA((splits + WINDOW,)),
        ],
        compiler_params=pltpu.CompilerParams(vmem_limit_bytes=VMEM_LIMIT),
        cost_estimate=pl.CostEstimate(
            flops=16 * 2 * 5 * TILES * stretch * stretch * heads * HEAD_SIZE // 4,
            bytes_accessed=1 << 22,
            transcendentals=0,
        ),
    )(ids, *chunk, *blocks)
    return out[:splits] if go_apart else out[0], out[-WINDOW:]


def from_columns(z, arrays, starts, width, apart):
    rows, count = arrays[0].shape[0], len(starts(0))
    shape = (len(arrays), rows, width)

    def kernel(z_ref, *refs):
        array_refs, out_refs, sem_ref = refs[: len(arrays)], refs[len(arrays) : -1], refs[-1]
        copies = []
        for i, start in enumerate(starts(z_ref[0])):
            at = pl.ds(pl.multiple_of(start, HEAD_SIZE), width)
            out = out_refs[i] if apart else out_refs[0].at[i]
            copies += [
                pltpu.make_async_copy(array.at[:, at], out.at[k], sem_ref.at[i, k])
                for k, array in enumerate(array_refs)
            ]
        for copy in copies:
            copy.start()
        for copy in copies:
            copy.wait()

    shapes = [shape] * count if apart else [(count,) + shape]
    return pl.pallas_call(
        kernel,
        in_specs=[pl.BlockSpec(memory_space=pltpu.SMEM)]
        + [pl.BlockSpec(memory_space=pl.ANY)] * len(arrays),
        out_specs=[pl.BlockSpec(memory_space=pltpu.VMEM)] * len(shapes),
        out_shape=[jax.ShapeDtypeStruct(one, LOW) for one in shapes],
        scratch_shapes=[pltpu.SemaphoreType.DMA((count, len(arrays)))],
        compiler_params=pltpu.CompilerParams(vmem_limit_bytes=8 * 1024 * 1024),
    )(z.astype(jnp.int32)[None], *arrays)


def in_columns(parts, z, places, outs):
    rows = parts[0].shape[-2]

    def kernel(z_ref, *refs):
        part_refs, out_refs = refs[: len(parts)], refs[len(parts) :]
        for index, part in enumerate(part_refs):
            for piece, out, column in places(z_ref[0], index, part):
                width = piece.shape[-1]
                start = pl.multiple_of(column * width, HEAD_SIZE)
                out_refs[out][:, pl.ds(start, width)] = piece

    size = sum(part.size for part in parts) // rows // outs
    return pl.pallas_call(
        kernel,
        in_specs=[pl.BlockSpec(memory_space=pltpu.SMEM)]
        + [pl.BlockSpec(memory_space=pltpu.VMEM)] * len(parts),
        out_specs=[pl.BlockSpec(memory_space=pltpu.VMEM)] * outs,
        out_shape=[jax.ShapeDtypeStruct((rows, size), LOW)] * outs,
        compiler_params=pltpu.CompilerParams(vmem_limit_bytes=8 * 1024 * 1024),
    )(z.astype(jnp.int32)[None], *parts)


def body(query, key, value, d_out, stretch_ids):
    rows = query.shape[0]
    ranks = lax.axis_size("ctx")
    splits = lax.axis_size("head")
    local = KEY_VALUE_HEADS // splits
    z = lax.axis_index("head")
    rank = lax.axis_index("ctx")
    fence = lax.optimization_barrier

    def shift(array, axis, by):
        size = lax.axis_size(axis)
        return lax.ppermute(array, axis, [(i, (i + by) % size) for i in range(size)])

    def exchange(chunks, sign):
        return [chunks[0]] + [shift(chunks[s], "head", sign * s) for s in range(1, splits)]

    def swap(array):
        return lax.all_to_all(array, "head", split_axis=0, concat_axis=0, tiled=True)

    def ids_of(turn):
        source = lax.rem(rank - turn + ranks, ranks)
        return lax.dynamic_slice_in_dim(stretch_ids, 2 * source, 2)

    ids = jnp.concatenate([ids_of(t) for t in range(WINDOW)] + [z.astype(jnp.int32)[None]])

    def for_device_ahead(s):
        start = lax.rem(z + s, splits) * (local * HEAD_SIZE)
        ahead = [
            lax.dynamic_slice_in_dim(array, start, local * HEAD_SIZE, 1) for array in (key, value)
        ]
        return jnp.concatenate(
            [
                array[:, j * HEAD_SIZE : (j + 1) * HEAD_SIZE]
                for j in range(local)
                for array in ahead
            ],
            axis=1,
        )

    parts = exchange([for_device_ahead(s) for s in range(splits)], 1)
    group = GROUP * HEAD_SIZE

    def in_order(j):
        def starts(_):
            return [(g * local + j) * group for g in range(splits)]

        return from_columns(z, (query, d_out), starts, group, False)[0]

    def apart(j):
        def starts(place):
            return [(lax.rem(place + s, splits) * local + j) * group for s in range(splits)]

        return from_columns(z, (query, d_out), starts, group, True)

    near = [s for s in range(1, splits) if 2 * s != splits]
    both = [in_order(0)] + [apart(j) for j in range(1, local)]
    *both, came = fence((*both, [parts[s] for s in near]))
    for s, part in zip(near, came):
        parts[s] = part

    blocks = [jnp.stack(parts)]
    for _ in range(1, WINDOW):
        blocks.append(shift(blocks[-1], "ctx", 1))
    chunks = [swap(both[0])]
    for j in range(1, local):
        both[j], chunks[j - 1] = fence((both[j], chunks[j - 1]))
        chunks.append(exchange(both[j], 1))

    def home(dkv):
        return [dkv[0]] + [shift(dkv[t], "ctx", -t) for t in range(1, WINDOW)]

    def add(dkv):
        return sum(d.astype(WIDE) for d in dkv).astype(LOW)

    dq, dkv = [], []
    for j in range(local):
        last = j > 0 and j == local - 1
        dq_j, dkv_j = attention(ids, chunks[j], blocks, j, last)
        if j + 1 < local:
            came = chunks[j + 1]
            came = [came[s] for s in near]
            dq_j, came = fence((dq_j, came))
            for s, part in zip(near, came):
                chunks[j + 1][s] = part
        if j > 0:
            dkv_j, dkv[j - 1] = fence((dkv_j, dkv[j - 1]))
            dq_j, dq[j - 1] = fence((dq_j, dq[j - 1]))
        dq.append(exchange(dq_j, -1) if last else swap(dq_j))
        dkv.append(home(dkv_j))

    dkv = jnp.stack([add(d) for d in dkv], axis=1)
    dkv, dq[-1] = fence((dkv, dq[-1]))
    dkv = exchange(list(dkv), -1)
    columns, pieces = [], []
    for j, part in enumerate(dq):
        if isinstance(part, list):
            columns += [[(s, j, None)] for s in range(splits)]
            pieces += part
        else:
            columns.append([(g, j, g) for g in range(splits)])
            pieces.append(part)
    dq = in_columns(
        pieces,
        z,
        lambda z, index, part: [
            (part[...], 0, lax.rem(z + s, splits) * local + j)
            if g is None
            else (part[g], 0, g * local + j)
            for s, j, g in columns[index]
        ],
        1,
    )
    dq, dkv = fence((dq, dkv))
    dk, dv = in_columns(
        dkv,
        z,
        lambda z, s, part: [
            (
                part[j, :, i * HEAD_SIZE : (i + 1) * HEAD_SIZE],
                i,
                lax.rem(z + s, splits) * local + j,
            )
            for j in range(local)
            for i in range(2)
        ],
        2,
    )
    return dq[0], dk, dv


def solution(mesh):
    spec = P(("ctx", "head"), None)
    return jax.shard_map(
        body,
        mesh=mesh,
        in_specs=(spec, spec, spec, spec, P()),
        out_specs=(spec, spec, spec),
        check_vma=False,
    )
```
